128 devices in a mesh: row: 8 (over y, core), col: 16 (over x, z).
Axes of the slice: x: 4, y: 4, z: 4, core: 2. Of those that a mesh axis runs over, the one named last changes fastest.
Arguments:
- kernel: float32 [8, 2048, 4, 4096], P(None, 'row', None, 'col'), may hold values from 0 to 8, as said below
Outputs:
- factored: float32 [8, 2048, 4, 4096], P(None, 'row', None, 'col')
The draws below stay inside these ranges and needn't reach their ends.
Inputs may be any that keep to these rules, and one draw needn't show every extreme that they name: `kernel`: symmetric positive definite.
All inputs are finite; a program needn't handle non-finite values.
Results may differ from the reference program's by a relative error of at most 0.0003.
Values sent between devices are 32-bit elements; how exact they have to be, the bound alone decides.
A program may use at most 192 MiB of HBM per device.

```python
import jax
import jax.numpy as jnp
from jax import lax

M = 16384
NB = 1024
RT = 8
CT = 4


def draw_kernel(key, part):
    key = jax.random.fold_in(key, 1)
    key_feat, key_len, key_jit = jax.random.split(key, 3)
    features = jax.random.uniform(key_feat, (M, 6), jnp.float32)
    amplitude = jnp.ones((M,), jnp.float32)
    base_length = 1.5 * float(M) ** (-1.0 / 6.0)
    lengths = base_length * jnp.exp(jax.random.uniform(key_len, (6,), jnp.float32, -0.3, 0.3))
    distance = jnp.zeros((M, M), jnp.float32)
    for feature in range(6):
        spread = (features[:, None, feature] - features[None, :, feature]) / lengths[feature]
        distance = distance + spread * spread
    jitter = jax.random.uniform(key_jit, (M,), jnp.float32, 0.3, 0.6)
    indices = jnp.arange(M)
    diagonal = indices[:, None] == indices[None, :]
    values = jnp.exp(-0.5 * jnp.minimum(distance, 160.0)) + jnp.where(diagonal, jitter[:, None], 0.0)
    values = 0.001 * amplitude[:, None] * amplitude[None, :] * values
    return values.reshape(RT, M // RT, CT, M // CT)


def setup_inputs(seed: int = 0) -> dict:
    streams_of = jax.random.split(jax.random.key(seed), 2)
    kernel = draw_kernel(jax.random.fold_in(streams_of[1], 71), 0)
    return {"kernel": kernel}


def reference(kernel):
    whole = kernel.reshape(M, M)
    lead = whole[:NB, :NB]
    lower_factor = jnp.linalg.cholesky(lead)
    below = whole[NB:, :NB]
    panel_rows = lax.linalg.triangular_solve(lower_factor, below, left_side=False, lower=True, transpose_a=True)
    product = jnp.dot(panel_rows.astype(jnp.float32), panel_rows.T.astype(jnp.float32), precision=lax.Precision.HIGHEST, preferred_element_type=jnp.float32)
    schur = whole[NB:, NB:] - product
    top = jnp.concatenate([lower_factor, jnp.zeros((NB, M - NB), jnp.float32)], axis=1)
    bottom = jnp.concatenate([panel_rows, schur], axis=1)
    result = jnp.concatenate([top, bottom], axis=0)
    return result.reshape(RT, M // RT, CT, M // CT)
```

```python
import functools

import jax
import jax.numpy as jnp
from jax import lax
from jax.experimental import pallas as pl
from jax.experimental.pallas import tpu as pltpu
from jax.sharding import PartitionSpec as P

F32=jnp.float32; BF=jnp.bfloat16

def split(a):
    hi=a.astype(BF)
    return hi,(a-hi.astype(F32)).astype(BF)
NN=(((1,),(0,)),((),())); NT=(((1,),(1,)),((),())); TN=(((0,),(0,)),((),()))
def dot3(a,b,dims=NN):
    d=functools.partial(lax.dot_general,dimension_numbers=dims,preferred_element_type=F32)
    return d(a[0],b[0])+(d(a[0],b[1])+d(a[1],b[0]))

def finish_kernel(pos,ker,rows,cols,u_ref,w_ref,out,uh,ul,wh,wl,yh,yl,xh,xl,xp):
    t=pl.program_id(0); r=pos[0]; c=pos[1]
    T=256
    @pl.when(t==0)
    def _():
        for k in range(4):
            uh[k*T:(k+1)*T,:],ul[k*T:(k+1)*T,:]=split(u_ref[k*T:(k+1)*T,:])
            wh[k],wl[k]=split(w_ref[k])
        for k in range(4):
            acc=cols[k*T:(k+1)*T,:]
            for j in range(k):
                acc=acc-dot3((uh[j*T:(j+1)*T,k*T:(k+1)*T],ul[j*T:(j+1)*T,k*T:(k+1)*T]),(yh[j*T:(j+1)*T,:],yl[j*T:(j+1)*T,:]),TN)
            y=dot3((wh[k],wl[k]),split(acc))
            yh[k*T:(k+1)*T,:],yl[k*T:(k+1)*T,:]=split(y)
    lead=jnp.logical_and(t==0,r<4)
    @pl.when(lead)
    def _():
        out[...]=jnp.zeros_like(out)
        @pl.when(c<4)
        def _():
            blk=u_ref[pl.ds(pl.multiple_of(jnp.minimum(c,3)*T,T),T),pl.ds(pl.multiple_of(jnp.minimum(r,3)*T,T),T)]
            out[0,:,0,:]=blk.T
    @pl.when(jnp.logical_not(lead))
    def _():
        for k in range(4):
            ks=slice(k*T,(k+1)*T)
            acc=rows[:,ks]
            for j in range(k):
                js=slice(j*T,(j+1)*T)
                acc=acc-dot3((xh[:,js],xl[:,js]),(uh[js,ks],ul[js,ks]))
            x=dot3(split(acc),(wh[k],wl[k]),NT)
            xh[:,ks],xl[:,ks]=split(x)
            xp[:,ks]=x
        for uu in range(4):
            us=slice(uu*T,(uu+1)*T)
            s=dot3((xh[...],xl[...]),(yh[:,us],yl[:,us]))
            out[0,:,uu,:]=ker[0,:,uu,:]-s
        @pl.when(c<4)
        def _():
            out[0,:,0,:]=xp[:,pl.ds(pl.multiple_of(jnp.minimum(c,3)*T,T),T)]

def finish(pos,kernel,rows,cols,u,w):
    full=lambda shape: pl.BlockSpec(shape,lambda t:(0,)*len(shape),pipeline_mode=pl.Buffered(1))
    return pl.pallas_call(finish_kernel,grid=(8,),
        in_specs=[pl.BlockSpec(memory_space=pltpu.SMEM),pl.BlockSpec((1,256,4,256),lambda t:(t,0,0,0)),
                  pl.BlockSpec((256,1024),lambda t:(t,0)),full((1024,1024)),full((1024,1024)),full((4,256,256))],
        out_specs=pl.BlockSpec((1,256,4,256),lambda t:(t,0,0,0)),
        out_shape=jax.ShapeDtypeStruct((8,256,4,256),F32),
        scratch_shapes=[pltpu.VMEM((1024,1024),BF)]*2+[pltpu.VMEM((4,256,256),BF)]*2+[pltpu.VMEM((1024,1024),BF)]*2+[pltpu.VMEM((256,1024),BF)]*2+[pltpu.VMEM((256,1024),F32)],
        compiler_params=pltpu.CompilerParams(vmem_limit_bytes=56<<20),name="finish")(pos,kernel,rows,cols,u,w)

HI=lax.Precision.HIGHEST
def bc(x,i,n=8): return jnp.broadcast_to(x[i:i+1,:],(n,x.shape[1]))
def dotx(a,b,dims=NN): return lax.dot_general(a,b,dims,precision=HI,preferred_element_type=F32)
def leaf(V, c0, b, u_ref, w_ref, r0, mb):
    nt=b//8; mt=mb//8
    VT=[[V[8*t:8*t+8,128*h:128*h+128] for h in range(2)] for t in range(nt)]
    refs=[u_ref,w_ref]
    for s in range(0,nt,mt):
        C=[[jnp.broadcast_to(VT[t][0][:, c0+8*s+j:c0+8*s+j+1],(8,128)) if t>=s+j//8 else None for t in range(nt)] for j in range(mb)]
        d=bc(C[0][s],0)
        for k in range(mb):
            tk=s+k//8
            ck=C[k]
            q=pltpu.reciprocal(d,approx=False)
            rs=lax.rsqrt(d)
            if k+1<mb:
                sb=bc(ck[s+(k+1)//8],(k+1)%8)
                p=bc(C[k+1][s+(k+1)//8],(k+1)%8)
                d=p-(sb*sb)*q
            m=[ck[t]*q if t>=tk else None for t in range(nt)]
            v=[bc(VT[tk][h],k%8) for h in range(2)]
            for h in range(2): refs[h][r0+8*s+k:r0+8*s+k+1,:]=(v[h]*rs)[:1]
            for j in range(k+1,mb):
                cj=bc(ck[s+j//8],j%8)
                for t in range(s+j//8,nt):
                    C[j][t]=C[j][t]-m[t]*cj
            for t in range(s+(k+1)//8,nt):
                for h in range(2):
                    VT[t][h]=VT[t][h]-m[t]*v[h]
def iotas(n,m):
    return lax.broadcasted_iota(jnp.int32,(n,m),0),lax.broadcasted_iota(jnp.int32,(n,m),1)
def block128(D,us,ws,b=32,mb=16):
    ii,jj=iotas(128,128)
    I=(ii==jj).astype(F32)
    for s in range(128//b):
        r0=s*b
        V=jnp.concatenate([D[r0:r0+b],I[r0:r0+b]],axis=1)
        if s:
            up=us[:r0,:]; wp=ws[:r0,:]
            V=V-dotx(up[:,r0:r0+b], jnp.concatenate([up,wp],axis=1),TN)
        leaf(V,r0,b,us,ws,r0,mb)

def chol_loop(u,w,us,ws):
    B=128
    def step(k,_):
        ko=pl.multiple_of(k*B,B)
        block128(u[pl.ds(ko,B),pl.ds(ko,B)],us,ws)
        ii,jj=iotas(B,B)
        W=jnp.where(jj<=ii,ws[...],0.0)
        ws[...]=W
        ri,ci=iotas(B,1024)
        U=jnp.where(ci>=ri+ko,dotx(W,u[pl.ds(ko,B),:]),0.0)
        u[pl.ds(ko,B),:]=U
        def upd(j,_):
            jo=pl.multiple_of(j*B,B)
            u[pl.ds(jo,B),:]=u[pl.ds(jo,B),:]-dotx(u[pl.ds(ko,B),pl.ds(jo,B)],U_ref[...] if False else u[pl.ds(ko,B),:],TN)
            return 0
        lax.fori_loop(k+1,8,upd,0)
        h=k//2
        @pl.when(k%2==0)
        def _():
            w[pl.ds(h,1),:B,:B]=W[None]
            w[pl.ds(h,1),:B,B:]=jnp.zeros((1,B,B),F32)
        @pl.when(k%2==1)
        def _():
            W1=w[pl.ds(h,1),:B,:B][0]
            kp=pl.multiple_of(ko-B,B)
            L21=dotx(u[pl.ds(kp,B),pl.ds(ko,B)],W1,TN)
            w[pl.ds(h,1),B:,B:]=W[None]
            w[pl.ds(h,1),B:,:B]=-dotx(W,L21)[None]
        return 0
    lax.fori_loop(0,8,step,0)
def chol_kernel(a_ref,u,w,us,ws):
    u[...]=a_ref[...]
    chol_loop(u,w,us,ws)
def chol(a):
    return pl.pallas_call(chol_kernel,out_shape=[jax.ShapeDtypeStruct((1024,1024),F32),jax.ShapeDtypeStruct((4,256,256),F32)],
        in_specs=[pl.BlockSpec(memory_space=pltpu.VMEM)],out_specs=[pl.BlockSpec(memory_space=pltpu.VMEM)]*2,
        scratch_shapes=[pltpu.VMEM((128,128),F32)]*2,compiler_params=pltpu.CompilerParams(vmem_limit_bytes=48<<20),name="factor")(a)

def from_first_four(x, pieces):
    n=x.shape[0]//4
    xs=x.reshape(4,n,x.shape[1])
    c=lax.axis_index("col")
    got=xs[0]
    for d in (1,2,3):
        g=lax.ppermute(xs[d],"col",[(z,4*d+z) for z in range(4)])
        got=jnp.where(c//4==d,g,got)
    allp=lax.all_gather(got,"col",axis=0)
    return allp.reshape(4,4,n,x.shape[1]).transpose(1,0,2,3).reshape(4,4*n,x.shape[1])


def per_device(kernel):
    r=lax.axis_index("row"); c=lax.axis_index("col")
    pcol=kernel[:,:,0,:].reshape(2048,256)
    strip=kernel[0].transpose(1,0,2)
    half=strip.reshape(4,2,128,256)
    g=lax.ppermute(half[:,1],"row",[(i,i+4) for i in range(4)])
    piece=jnp.where(r<4,half[:,0],g)
    gat=lax.all_gather(piece,"row",axis=0)
    cols=gat.reshape(2,4,4,128,256).transpose(1,0,3,2,4).reshape(1024,1024)
    lead=from_first_four(cols[:,:256],4).transpose(1,0,2).reshape(1024,1024)
    rows=from_first_four(pcol,4).transpose(1,0,2).reshape(2048,1024)
    u,w=chol(lead)
    pos=jnp.stack([r,c]).astype(jnp.int32)
    return finish(pos,kernel,rows,cols,u,w)


def solution(mesh):
    spec=P(None,"row",None,"col")
    return jax.shard_map(per_device,mesh=mesh,in_specs=(spec,),out_specs=spec,check_vma=False)
```

```python
import functools

import jax
import jax.numpy as jnp
from jax import lax
from jax.experimental import pallas as pl
from jax.experimental.pallas import tpu as pltpu
from jax.sharding import PartitionSpec as P

F32=jnp.float32; BF=jnp.bfloat16

def split(a):
    hi=a.astype(BF)
    return hi,(a-hi.astype(F32)).astype(BF)
NN=(((1,),(0,)),((),())); NT=(((1,),(1,)),((),())); TN=(((0,),(0,)),((),()))
def dot3(a,b,dims=NN):
    d=functools.partial(lax.dot_general,dimension_numbers=dims,preferred_element_type=F32)
    return d(a[0],b[0])+(d(a[0],b[1])+d(a[1],b[0]))

def finish_kernel(pos,ker,rows,cols,u_ref,w_ref,out,uh,ul,wh,wl,yh,yl,xh,xl,xp):
    t=pl.program_id(0); r=pos[0]; c=pos[1]
    T=256
    @pl.when(t==0)
    def _():
        for k in range(4):
            uh[k*T:(k+1)*T,:],ul[k*T:(k+1)*T,:]=split(u_ref[k*T:(k+1)*T,:])
            wh[k],wl[k]=split(w_ref[k])
        for k in range(4):
            acc=jnp.concatenate([cols[k,uu] for uu in range(4)],axis=1)
            for j in range(k):
                acc=acc-dot3((uh[j*T:(j+1)*T,k*T:(k+1)*T],ul[j*T:(j+1)*T,k*T:(k+1)*T]),(yh[j*T:(j+1)*T,:],yl[j*T:(j+1)*T,:]),TN)
            y=dot3((wh[k],wl[k]),split(acc))
            yh[k*T:(k+1)*T,:],yl[k*T:(k+1)*T,:]=split(y)
    lead=jnp.logical_and(t==0,r<4)
    @pl.when(lead)
    def _():
        out[...]=jnp.zeros_like(out)
        @pl.when(c<4)
        def _():
            blk=u_ref[pl.ds(pl.multiple_of(jnp.minimum(c,3)*T,T),T),pl.ds(pl.multiple_of(jnp.minimum(r,3)*T,T),T)]
            out[0,:,0,:]=blk.T
    @pl.when(jnp.logical_not(lead))
    def _():
        for k in range(4):
            ks=slice(k*T,(k+1)*T)
            acc=rows[k]
            for j in range(k):
                js=slice(j*T,(j+1)*T)
                acc=acc-dot3((xh[:,js],xl[:,js]),(uh[js,ks],ul[js,ks]))
            x=dot3(split(acc),(wh[k],wl[k]),NT)
            xh[:,ks],xl[:,ks]=split(x)
            xp[:,ks]=x
        for uu in range(4):
            us=slice(uu*T,(uu+1)*T)
            s=dot3((xh[...],xl[...]),(yh[:,us],yl[:,us]))
            out[0,:,uu,:]=ker[0,:,uu,:]-s
        @pl.when(c<4)
        def _():
            out[0,:,0,:]=xp[:,pl.ds(pl.multiple_of(jnp.minimum(c,3)*T,T),T)]

def finish(pos,kernel,rows,cols,u,w):
    full=lambda shape: pl.BlockSpec(shape,lambda t:(0,)*len(shape),pipeline_mode=pl.Buffered(1))
    return pl.pallas_call(finish_kernel,grid=(8,),
        in_specs=[pl.BlockSpec(memory_space=pltpu.SMEM),pl.BlockSpec((1,256,4,256),lambda t:(t,0,0,0)),
                  pl.BlockSpec((4,256,256),lambda t:(0,t,0)),full((4,4,256,256)),full((1024,1024)),full((4,256,256))],
        out_specs=pl.BlockSpec((1,256,4,256),lambda t:(t,0,0,0)),
        out_shape=jax.ShapeDtypeStruct((8,256,4,256),F32),
        scratch_shapes=[pltpu.VMEM((1024,1024),BF)]*2+[pltpu.VMEM((4,256,256),BF)]*2+[pltpu.VMEM((1024,1024),BF)]*2+[pltpu.VMEM((256,1024),BF)]*2+[pltpu.VMEM((256,1024),F32)],
        compiler_params=pltpu.CompilerParams(vmem_limit_bytes=56<<20),name="finish")(pos,kernel,rows,cols,u,w)

HI=lax.Precision.HIGHEST
def bc(x,i,n=8): return jnp.broadcast_to(x[i:i+1,:],(n,x.shape[1]))
def dotx(a,b,dims=NN): return lax.dot_general(a,b,dims,precision=HI,preferred_element_type=F32)
def leaf(V, c0, b, u_ref, w_ref, r0, mb):
    nt=b//8; mt=mb//8
    VT=[[V[8*t:8*t+8,128*h:128*h+128] for h in range(2)] for t in range(nt)]
    refs=[u_ref,w_ref]
    for s in range(0,nt,mt):
        C=[[jnp.broadcast_to(VT[t][0][:, c0+8*s+j:c0+8*s+j+1],(8,128)) if t>=s+j//8 else None for t in range(nt)] for j in range(mb)]
        d=bc(C[0][s],0)
        for k in range(mb):
            tk=s+k//8
            ck=C[k]
            q=pltpu.reciprocal(d,approx=False)
            rs=lax.rsqrt(d)
            if k+1<mb:
                sb=bc(ck[s+(k+1)//8],(k+1)%8)
                p=bc(C[k+1][s+(k+1)//8],(k+1)%8)
                d=p-(sb*sb)*q
            m=[ck[t]*q if t>=tk else None for t in range(nt)]
            v=[bc(VT[tk][h],k%8) for h in range(2)]
            for h in range(2): refs[h][r0+8*s+k:r0+8*s+k+1,:]=(v[h]*rs)[:1]
            for j in range(k+1,mb):
                cj=bc(ck[s+j//8],j%8)
                for t in range(s+j//8,nt):
                    C[j][t]=C[j][t]-m[t]*cj
            for t in range(s+(k+1)//8,nt):
                for h in range(2):
                    VT[t][h]=VT[t][h]-m[t]*v[h]
def iotas(n,m):
    return lax.broadcasted_iota(jnp.int32,(n,m),0),lax.broadcasted_iota(jnp.int32,(n,m),1)
def block128(D,us,ws,b=32,mb=16):
    ii,jj=iotas(128,128)
    I=(ii==jj).astype(F32)
    for s in range(128//b):
        r0=s*b
        V=jnp.concatenate([D[r0:r0+b],I[r0:r0+b]],axis=1)
        if s:
            up=us[:r0,:]; wp=ws[:r0,:]
            V=V-dotx(up[:,r0:r0+b], jnp.concatenate([up,wp],axis=1),TN)
        leaf(V,r0,b,us,ws,r0,mb)


T=256


def flip(dim, x, z):
    if dim==0: return x+1-2*lax.rem(x,2),z
    if dim==1: return x,z+1-2*lax.rem(z,2)
    if dim==2: return 3-x,z
    return x,3-z


def orbit(dims, x, z):
    out=[(x,z)]
    for d in dims:
        out=out+[flip(d,a,b) for a,b in out]
    return out


class Traffic:
    def __init__(self, send_sems, recv_sems):
        self.send_sems=send_sems; self.recv_sems=recv_sems
        self.sent=[]; self.keys={}; self.next=0

    def slots(self, key, n):
        if key not in self.keys:
            self.keys[key]=self.next
            self.next+=n
        return self.keys[key]

    def send(self, cond, src, dst, sem, row, col):
        d=pltpu.make_async_remote_copy(src_ref=src,dst_ref=dst,send_sem=self.send_sems.at[len(self.sent)],recv_sem=self.recv_sems.at[sem],
            device_id={"row":row,"col":col},device_id_type=pl.DeviceIdType.MESH)
        if cond is None: d.start()
        else: pl.when(cond)(lambda: d.start())
        self.sent.append((cond,d))
        return len(self.sent)-1

    def settle(self, n, cond):
        c,d=self.sent[n]
        pl.when(both(c,cond))(lambda: d.wait_send())

    def local(self, cond, src, dst):
        d=pltpu.make_async_copy(src,dst,self.send_sems.at[len(self.sent)])
        if cond is None: d.start()
        else: pl.when(cond)(lambda: d.start())
        self.sent.append((None,None))
        def wait():
            if cond is None: d.wait()
            else: pl.when(cond)(lambda: d.wait())
        return wait

    def recv(self, cond, dst, sem):
        d=pltpu.make_async_copy(dst,dst,self.recv_sems.at[sem])
        if cond is None: d.wait()
        else: pl.when(cond)(lambda: d.wait())

    def drain(self, settled):
        for n,(cond,d) in enumerate(self.sent):
            if d is None or n in settled: continue
            if cond is None: d.wait_send()
            else: pl.when(cond)(lambda d=d: d.wait_send())


def both(a,b):
    return b if a is None else jnp.logical_and(a,b)


def gather_factor_kernel(panel,strip,row_out,col_out,u,w,us,ws,stage,send_sems,recv_sems):
    r=lax.axis_index("row"); c=lax.axis_index("col")
    y=r//2; core=lax.rem(r,2); x=c//4; z=lax.rem(c,4)
    up=lambda v,n=1: lax.rem(v+n,4)
    at=lambda yy,kk,xx,zz: (2*yy+kk,4*xx+zz)
    tr=Traffic(send_sems,recv_sems)
    bar=pltpu.get_barrier_semaphore()
    friends=[at(up(y,i),core,x,z) for i in (1,3)]+[at(y,1-core,x,z)]+[at(y,core,up(x,i),z) for i in (1,3)]+[at(y,core,x,up(z,i)) for i in (1,3)]
    for a,b in friends:
        pl.semaphore_signal(bar,inc=1,device_id={"row":a,"col":b},device_id_type=pl.DeviceIdType.MESH)
    pl.semaphore_wait(bar,len(friends))

    tile=lambda k,U: u.at[pl.ds(pl.multiple_of(k*T,T),T),pl.ds(pl.multiple_of(U*T,T),T)]
    rs=jnp.minimum(r,3)
    B=tr.slots("B",8); BD=tr.slots("BD",8)
    low=y<2
    own=[]
    def b_first(q):
        own.append(tr.local(low,strip.at[q],col_out.at[rs,q]))
        for i in (1,3):
            a,b=at(up(y,i),core,x,z)
            tr.send(low,strip.at[q],col_out.at[rs,q],B+jnp.minimum(y,1)*4+q,a,b)
    b_first(0)
    x0=x==0; x13=lax.rem(x,2)==1; x2=x==2
    rowpart=lambda xx,zz,o,n: row_out.at[zz,pl.ds(pl.multiple_of(xx*512+o,128),n),:]
    CS=tr.slots("CS",1); CST=tr.slots("CST",1); CSF=tr.slots("CSF",2)
    for xx,h in ((1,0),(3,1)):
        a,b=at(y,core,xx,z)
        tr.send(x0,panel.at[1024+256*h:1280+256*h,:],stage,CST,a,b)
    for xx in (1,3):
        a,b=at(y,core,xx,z)
        tr.send(x0,panel.at[512*xx:512*xx+512,:],rowpart(xx,z,0,512),CS,a,b)
    crow=tr.local(x0,panel.at[0:512,:],rowpart(0,z,0,512))
    for q in (1,2,3): b_first(q)

    def b_forward(q):
        f=jnp.clip(3-y,0,1)
        tr.recv(y>=2,col_out.at[2*f+core,q],B+f*4+q)
        a,b=at(jnp.clip(5-y,0,3),core,x,z)
        tr.send(y>=2,col_out.at[2*f+core,q],col_out.at[2*f+core,q],B+f*4+q,a,b)
    def b_last(q):
        o=jnp.where(y>=2,y-2,1-y)
        tr.recv(None,col_out.at[2*o+core,q],B+o*4+q)
        own[q]()
    def b_share(q):
        a,b=at(y,1-core,x,z)
        for j in (0,1):
            tr.send(None,col_out.at[2*j+core,q],col_out.at[2*j+core,q],BD+j*4+q,a,b)
    def b_done(q):
        for j in (0,1):
            tr.recv(None,col_out.at[2*j+1-core,q],BD+j*4+q)
    b_forward(0); b_last(0)

    AX=tr.slots("AX",2); AZ=tr.slots("AZ",4); AF=tr.slots("AF",2); AD=tr.slots("AD",8)
    kk=lambda j: 2*j+core
    need=lambda j,U: U>=kk(j)
    lead_own=[]; lead_sent=[[],[]]
    for j in (0,1):
        ok=jnp.logical_and(x0,need(j,z))
        for xx in (1,3):
            a,b=at(y,core,xx,z)
            tr.send(ok,col_out.at[kk(j),0],tile(kk(j),z),AX+j,a,b)
        lead_own.append(tr.local(ok,col_out.at[kk(j),0],tile(kk(j),z)))
    for j,xx in ((0,1),(1,3)):
        ok=jnp.logical_and(x==xx,need(j,z))
        tr.recv(ok,tile(kk(j),z),AX+j)
        a,b=at(y,core,2,z)
        lead_sent[j].append(tr.send(ok,tile(kk(j),z),tile(kk(j),z),AX+j,a,b))
    for j,xx in ((0,1),(1,3)):
        lead_own[j]()
        tr.recv(jnp.logical_and(jnp.logical_and(x!=0,x!=xx),need(j,z)),tile(kk(j),z),AX+j)
    for j in (0,1):
        ok=need(j,z)
        for e,i in ((0,1),(1,3)):
            a,b=at(y,core,x,up(z,i))
            lead_sent[j].append(tr.send(ok,tile(kk(j),z),tile(kk(j),z),AZ+2*e+j,a,b))
        a,b=at(y,1-core,x,z)
        lead_sent[j].append(tr.send(ok,tile(kk(j),z),tile(kk(j),z),AD+j*4,a,b))
    tr.recv(x13,stage,CST)
    a,b=at(y,core,2,z)
    h=jnp.where(x==3,1,0)
    tr.send(x13,stage,row_out.at[z,pl.ds(pl.multiple_of(1024+256*h,256),256),:],CSF+h,a,b)
    for e,i in ((0,3),(1,1)):
        U=up(z,i)
        for j in (0,1):
            ok=need(j,U)
            tr.recv(ok,tile(kk(j),U),AZ+2*e+j)
            if e==j:
                a,b=at(y,core,x,up(z,1 if e==0 else 3))
                lead_sent[j].append(tr.send(ok,tile(kk(j),U),tile(kk(j),U),AF+j,a,b))
            a,b=at(y,1-core,x,z)
            lead_sent[j].append(tr.send(ok,tile(kk(j),U),tile(kk(j),U),AD+j*4+i,a,b))
    for j in (0,1):
        U=up(z,2); ok=need(j,U)
        tr.recv(ok,tile(kk(j),U),AF+j)
        a,b=at(y,1-core,x,z)
        lead_sent[j].append(tr.send(ok,tile(kk(j),U),tile(kk(j),U),AD+j*4+2,a,b))
    AG=tr.slots("AG",60)
    orders=[[(q+i)%4 for i in range(4)] for q in range(4)]
    def ag_send(i):
        for q in range(4):
            dims=orders[q]
            xx,zz=flip(dims[i],x,z)
            a,b=at(y,core,xx,zz)
            for m,(bx,bz) in enumerate(orbit(dims[:i],x,z)):
                ref=rowpart(bx,bz,128*q,128)
                tr.send(None,ref,ref,AG+q*15+(1<<i)-1+m,a,b)
    def ag_recv(i):
        for q in range(4):
            dims=orders[q]
            xx,zz=flip(dims[i],x,z)
            for m,(bx,bz) in enumerate(orbit(dims[:i],xx,zz)):
                tr.recv(None,rowpart(bx,bz,128*q,128),AG+q*15+(1<<i)-1+m)
    tr.recv(x13,rowpart(x,z,0,512),CS)
    for e in (0,1):
        tr.recv(x2,rowpart(x,z,256*e,256),CSF+e)
    crow()
    ag_send(0)
    settled=set()
    def lead_wait(k):
        mine=core==k%2
        for n in lead_sent[k//2]:
            tr.settle(n,mine)
            settled.add(n)
        for i in range(4):
            U=up(z,i)
            tr.recv(jnp.logical_and(jnp.logical_not(mine),U>=k),tile(k,U),AD+(k//2)*4+i)
    def more(n):
        if n==0:
            ag_recv(0); ag_send(1)
            for q in (1,2,3): b_forward(q)
        elif n==1:
            ag_recv(1); ag_send(2)
            for q in (0,1,2,3):
                if q: b_last(q)
                b_share(q)
        elif n==2:
            ag_recv(2); ag_send(3)
        elif n==7:
            ag_recv(3)
            for q in range(4): b_done(q)
    chol_events(u,w,us,ws,lead_wait,more)
    tr.drain(settled)


def chol_events(u,w,us,ws,lead_wait,more):
    H=128
    for K in range(4):
        ko=T*K
        lead_wait(K)
        if K:
            u[ko:ko+T,ko:]=u[ko:ko+T,ko:]-dotx(u[:ko,ko:ko+T],u[:ko,ko:],TN)
            u[ko:ko+T,:ko]=jnp.zeros((T,ko),F32)
        Ws=[]
        for h in range(2):
            o=ko+H*h
            block128(u[o:o+H,o:o+H],us,ws)
            ii,jj=iotas(H,H)
            W=jnp.where(jj<=ii,ws[...],0.0)
            n=1024-ko
            ri,ci=iotas(H,n)
            U=jnp.where(ci>=ri+H*h,dotx(W,u[o:o+H,ko:]),0.0)
            u[o:o+H,ko:]=U
            if h==0:
                u[o+H:o+T,ko:]=u[o+H:o+T,ko:]-dotx(U[:,H:T],U,TN)
                w[K,:H,:H]=W
                w[K,:H,H:]=jnp.zeros((H,H),F32)
                L21=dotx(U[:,H:T],W,TN)
            else:
                w[K,H:,H:]=W
                w[K,H:,:H]=-dotx(W,L21)
            more(2*K+h)


def gather_factor(panel,strip):
    any_=pl.BlockSpec(memory_space=pl.ANY); vm=pl.BlockSpec(memory_space=pltpu.VMEM)
    return pl.pallas_call(gather_factor_kernel,
        out_shape=[jax.ShapeDtypeStruct((4,2048,256),F32),jax.ShapeDtypeStruct((4,4,256,256),F32),
                   jax.ShapeDtypeStruct((1024,1024),F32),jax.ShapeDtypeStruct((4,256,256),F32)],
        in_specs=[any_,any_],out_specs=[any_,any_,vm,vm],
        scratch_shapes=[pltpu.VMEM((128,128),F32)]*2+[pltpu.VMEM((256,256),F32),pltpu.SemaphoreType.DMA((160,)),pltpu.SemaphoreType.DMA((112,))],
        compiler_params=pltpu.CompilerParams(vmem_limit_bytes=48<<20,collective_id=0,has_side_effects=True),name="gather_factor")(panel,strip)


def per_device(kernel):
    r=lax.axis_index("row"); c=lax.axis_index("col")
    panel=kernel[:,:,0,:].reshape(2048,256)
    strip=kernel[0].transpose(1,0,2)
    rows,cols,u,w=gather_factor(panel,strip)
    pos=jnp.stack([r,c]).astype(jnp.int32)
    return finish(pos,kernel,rows,cols,u,w)


def solution(mesh):
    spec=P(None,"row",None,"col")
    return jax.shard_map(per_device,mesh=mesh,in_specs=(spec,),out_specs=spec,check_vma=False)
```

```python
import functools

import jax
import jax.numpy as jnp
from jax import lax
from jax.experimental import pallas as pl
from jax.experimental.pallas import tpu as pltpu
from jax.sharding import PartitionSpec as P

F32=jnp.float32; BF=jnp.bfloat16; T=256

def split(a):
    hi=a.astype(BF)
    return hi,(a-hi.astype(F32)).astype(BF)
NN=(((1,),(0,)),((),())); NT=(((1,),(1,)),((),())); TN=(((0,),(0,)),((),()))
def dot3(a,b,dims=NN):
    d=functools.partial(lax.dot_general,dimension_numbers=dims,preferred_element_type=F32)
    return d(a[0],b[0])+(d(a[0],b[1])+d(a[1],b[0]))

def finish_kernel(pos,ker,rows,l_blk,uh,ul,wh,wl,yh,yl,out,xh,xl,xp):
    t=pl.program_id(0); r=pos[0]; c=pos[1]
    lead=jnp.logical_and(t==0,r<4)
    @pl.when(lead)
    def _():
        out[...]=jnp.zeros_like(out)
        @pl.when(c<4)
        def _():
            out[0,:,0,:]=l_blk[...]
    @pl.when(jnp.logical_not(lead))
    def _():
        for k in range(4):
            ks=slice(k*T,(k+1)*T)
            acc=rows[k]
            if k:
                acc=acc-dot3((xh[:,:k*T],xl[:,:k*T]),(uh[:k*T,ks],ul[:k*T,ks]))
            x=dot3(split(acc),(wh[k],wl[k]),NT)
            xh[:,ks],xl[:,ks]=split(x)
            xp[:,ks]=x
        for uu in range(4):
            us=slice(uu*T,(uu+1)*T)
            s=dot3((xh[...],xl[...]),(yh[:,us],yl[:,us]))
            out[0,:,uu,:]=ker[0,:,uu,:]-s
        @pl.when(c<4)
        def _():
            out[0,:,0,:]=xp[:,pl.ds(pl.multiple_of(jnp.minimum(c,3)*T,T),T)]


def finish(pos,kernel,rows,*rest):
    full=lambda a: pl.BlockSpec(a.shape,lambda t:(0,)*a.ndim,pipeline_mode=pl.Buffered(1))
    return pl.pallas_call(finish_kernel,grid=(8,),
        in_specs=[pl.BlockSpec(memory_space=pltpu.SMEM),pl.BlockSpec((1,256,4,256),lambda t:(t,0,0,0)),
                  pl.BlockSpec((4,256,256),lambda t:(0,t,0))]+[full(a) for a in rest],
        out_specs=pl.BlockSpec((1,256,4,256),lambda t:(t,0,0,0)),
        out_shape=jax.ShapeDtypeStruct((8,256,4,256),F32),
        scratch_shapes=[pltpu.VMEM((256,1024),BF)]*2+[pltpu.VMEM((256,1024),F32)],
        compiler_params=pltpu.CompilerParams(vmem_limit_bytes=56<<20),name="finish")(pos,kernel,rows,*rest)


HI=lax.Precision.HIGHEST
def bc(x,i,n=8): return jnp.broadcast_to(x[i:i+1,:],(n,x.shape[1]))
def dotx(a,b,dims=NN): return lax.dot_general(a,b,dims,precision=HI,preferred_element_type=F32)
def leaf(V, c0, b, u_ref, w_ref, r0, mb):
    nt=b//8; mt=mb//8
    VT=[[V[8*t:8*t+8,128*h:128*h+128] for h in range(2)] for t in range(nt)]
    refs=[u_ref,w_ref]
    for s in range(0,nt,mt):
        C=[[jnp.broadcast_to(VT[t][0][:, c0+8*s+j:c0+8*s+j+1],(8,128)) if t>=s+j//8 else None for t in range(nt)] for j in range(mb)]
        d=bc(C[0][s],0)
        for k in range(mb):
            tk=s+k//8
            ck=C[k]
            q=pltpu.reciprocal(d,approx=False)
            rs=lax.rsqrt(d)
            if k+1<mb:
                sb=bc(ck[s+(k+1)//8],(k+1)%8)
                p=bc(C[k+1][s+(k+1)//8],(k+1)%8)
                d=p-(sb*sb)*q
            m=[ck[t]*q if t>=tk else None for t in range(nt)]
            v=[bc(VT[tk][h],k%8) for h in range(2)]
            for h in range(2): refs[h][r0+8*s+k:r0+8*s+k+1,:]=(v[h]*rs)[:1]
            for j in range(k+1,mb):
                cj=bc(ck[s+j//8],j%8)
                for t in range(s+j//8,nt):
                    C[j][t]=C[j][t]-m[t]*cj
            for t in range(s+(k+1)//8,nt):
                for h in range(2):
                    VT[t][h]=VT[t][h]-m[t]*v[h]
def iotas(n,m):
    return lax.broadcasted_iota(jnp.int32,(n,m),0),lax.broadcasted_iota(jnp.int32,(n,m),1)
def block128(D,us,ws,b=32,mb=16):
    ii,jj=iotas(128,128)
    I=(ii==jj).astype(F32)
    for s in range(128//b):
        r0=s*b
        V=jnp.concatenate([D[r0:r0+b],I[r0:r0+b]],axis=1)
        if s:
            up=us[:r0,:]; wp=ws[:r0,:]
            V=V-dotx(up[:,r0:r0+b], jnp.concatenate([up,wp],axis=1),TN)
        leaf(V,r0,b,us,ws,r0,mb)


def flip(dim, x, z):
    if dim==0: return x+1-2*lax.rem(x,2),z
    if dim==1: return x,z+1-2*lax.rem(z,2)
    if dim==2: return 3-x,z
    return x,3-z


def orbit(dims, x, z):
    out=[(x,z)]
    for d in dims:
        out=out+[flip(d,a,b) for a,b in out]
    return out


class Traffic:
    def __init__(self, send_sems, recv_sems):
        self.send_sems=send_sems; self.recv_sems=recv_sems
        self.sent=[]; self.keys={}; self.next=0

    def slots(self, key, n):
        if key not in self.keys:
            self.keys[key]=self.next
            self.next+=n
        return self.keys[key]

    def send(self, cond, src, dst, sem, row, col):
        d=pltpu.make_async_remote_copy(src_ref=src,dst_ref=dst,send_sem=self.send_sems.at[len(self.sent)],recv_sem=self.recv_sems.at[sem],
            device_id={"row":row,"col":col},device_id_type=pl.DeviceIdType.MESH)
        if cond is None: d.start()
        else: pl.when(cond)(lambda: d.start())
        self.sent.append((cond,d))
        return len(self.sent)-1

    def settle(self, n, cond):
        c,d=self.sent[n]
        c=both(c,cond)
        if c is None: d.wait_send()
        else: pl.when(c)(lambda: d.wait_send())

    def local(self, cond, src, dst):
        d=pltpu.make_async_copy(src,dst,self.send_sems.at[len(self.sent)])
        if cond is None: d.start()
        else: pl.when(cond)(lambda: d.start())
        self.sent.append((None,None))
        def wait():
            if cond is None: d.wait()
            else: pl.when(cond)(lambda: d.wait())
        return wait

    def recv(self, cond, dst, sem):
        d=pltpu.make_async_copy(dst,dst,self.recv_sems.at[sem])
        if cond is None: d.wait()
        else: pl.when(cond)(lambda: d.wait())

    def drain(self, settled):
        for n,(cond,d) in enumerate(self.sent):
            if d is None or n in settled: continue
            if cond is None: d.wait_send()
            else: pl.when(cond)(lambda d=d: d.wait_send())


def both(a,b):
    return b if a is None else a if b is None else jnp.logical_and(a,b)


def gather_factor_kernel(panel,strip,row_out,l_out,uh,ul,wh,wl,yh,yl,u,w,col_out,us,ws,stage,send_sems,recv_sems):
    r=lax.axis_index("row"); c=lax.axis_index("col")
    y=r//2; core=lax.rem(r,2); x=c//4; z=lax.rem(c,4)
    up=lambda v,n=1: lax.rem(v+n,4)
    at=lambda yy,kk,xx,zz: (2*yy+kk,4*xx+zz)
    tr=Traffic(send_sems,recv_sems)
    bar=pltpu.get_barrier_semaphore()
    friends=[at(up(y,i),core,x,z) for i in (1,2,3)]+[at(y,1-core,x,z)]+[at(y,core,up(x,i),z) for i in (1,2,3)]+[at(y,core,x,up(z,i)) for i in (1,2,3)]
    for a,b in friends:
        pl.semaphore_signal(bar,inc=1,device_id={"row":a,"col":b},device_id_type=pl.DeviceIdType.MESH)
    pl.semaphore_wait(bar,len(friends))

    tile=lambda k,U,o=0,n=T: u.at[pl.ds(pl.multiple_of(k*T+o,n),n),pl.ds(pl.multiple_of(U*T,T),T)]
    rs=jnp.minimum(r,3)
    low=y<2
    x0=x==0; x13=lax.rem(x,2)==1; x2=x==2
    rowpart=lambda xx,zz,o,n: row_out.at[zz,pl.ds(pl.multiple_of(xx*512+o,128),n),:]
    kk=lambda j: 2*j+core
    parts=[[(0,0,256)],[(1,0,256),(2,0,256),(3,0,256)]]
    lead_sent=[[] for _ in range(4)]
    def pieces(g):
        for k,o,n in parts[g]:
            key=k*2+(1 if o else 0)
            yield k,o,n,core==k%2,"%d"%key
    def window(k,o,n,q):
        return u.at[pl.ds(pl.multiple_of(k*T+o+n//4*q,n//4),n//4),k*T:]
    def patch(k,o,n,q,U):
        return u.at[pl.ds(pl.multiple_of(k*T+o+n//4*q,n//4),n//4),pl.ds(pl.multiple_of(U*T,T),T)]
    own_lead=[[] for _ in parts]
    def lead_a(g):
        for k,o,n,ok,key in pieces(g):
            sem=tr.slots("LA"+key,1); m=n//4
            go=jnp.logical_and(jnp.logical_and(ok,x0),jnp.logical_and(y==k//2,z>=k))
            src=lambda q: strip.at[0,pl.ds(pl.multiple_of(o+m*q,m),m),:]
            for i in (1,2,3):
                a,b=at(up(y,i),core,x,z)
                tr.send(go,src(up(y,i)),patch(k,o,n,up(y,i),z),sem,a,b)
            own_lead[g].append(tr.local(go,src(y),patch(k,o,n,y,z)))
    def lead_b(g):
        for wait in own_lead[g]: wait()
        for k,o,n,ok,key in pieces(g):
            ref=patch(k,o,n,y,z)
            go=jnp.logical_and(ok,jnp.logical_and(x0,z>=k))
            tr.recv(jnp.logical_and(go,y!=k//2),ref,tr.slots("LA"+key,1))
            sem=tr.slots("LB"+key,1)
            for i in (1,2,3):
                a,b=at(y,core,i,z)
                lead_sent[k].append(tr.send(go,ref,ref,sem,a,b))
    def lead_c(g):
        for k,o,n,ok,key in pieces(g):
            ref=patch(k,o,n,y,z)
            go=jnp.logical_and(ok,z>=k)
            tr.recv(jnp.logical_and(go,x!=0),ref,tr.slots("LB"+key,1))
            sem=tr.slots("LC"+key,3)
            for i in (1,2,3):
                a,b=at(y,core,x,up(z,i))
                lead_sent[k].append(tr.send(go,ref,ref,sem+i-1,a,b))
    def lead_d(g):
        for k,o,n,ok,key in pieces(g):
            sem=tr.slots("LC"+key,3)
            for i in (1,2,3):
                U=up(z,4-i)
                tr.recv(jnp.logical_and(ok,U>=k),patch(k,o,n,y,U),sem+i-1)
            ref=window(k,o,n,y)
            sem=tr.slots("LD"+key,3); cs=tr.slots("LE"+key,4)
            for i in (1,2,3):
                a,b=at(up(y,i),core,x,z)
                lead_sent[k].append(tr.send(ok,ref,ref,sem+i-1,a,b))
            a,b=at(y,1-core,x,z)
            lead_sent[k].append(tr.send(ok,ref,ref,cs,a,b))
    def lead_e(g):
        for k,o,n,ok,key in pieces(g):
            sem=tr.slots("LD"+key,3); cs=tr.slots("LE"+key,4)
            for i in (1,2,3):
                ref=window(k,o,n,up(y,4-i))
                tr.recv(ok,ref,sem+i-1)
                a,b=at(y,1-core,x,z)
                lead_sent[k].append(tr.send(ok,ref,ref,cs+i,a,b))
    def lead_wait(g):
        for k,o,n,ok,key in pieces(g):
            cs=tr.slots("LE"+key,4)
            for i in range(4):
                tr.recv(jnp.logical_not(ok),window(k,o,n,up(y,4-i)),cs+i)
    def lead_free(K):
        for n in lead_sent[K]:
            tr.settle(n,None)
            settled.add(n)
    settled=set()

    B=tr.slots("B",8); BD=tr.slots("BD",8)
    own=[]
    def b_first(q):
        own.append(tr.local(low,strip.at[q],col_out.at[rs,q]))
        for i in (1,3):
            a,b=at(up(y,i),core,x,z)
            tr.send(low,strip.at[q],col_out.at[rs,q],B+jnp.minimum(y,1)*4+q,a,b)
    def b_forward(q):
        f=jnp.clip(3-y,0,1)
        tr.recv(y>=2,col_out.at[2*f+core,q],B+f*4+q)
        a,b=at(jnp.clip(5-y,0,3),core,x,z)
        tr.send(y>=2,col_out.at[2*f+core,q],col_out.at[2*f+core,q],B+f*4+q,a,b)
    def b_last(q):
        o=jnp.where(y>=2,y-2,1-y)
        tr.recv(None,col_out.at[2*o+core,q],B+o*4+q)
        own[q]()
    def b_share(q):
        a,b=at(y,1-core,x,z)
        for j in (0,1):
            tr.send(None,col_out.at[2*j+core,q],col_out.at[2*j+core,q],BD+j*4+q,a,b)
    def b_done(q):
        for j in (0,1):
            tr.recv(None,col_out.at[2*j+1-core,q],BD+j*4+q)

    CS=tr.slots("CS",4); CST=tr.slots("CST",4); CSF=tr.slots("CSF",4)
    crow={}
    def c_scatter(q):
        for xx in (1,3):
            a,b=at(y,core,xx,z)
            tr.send(x0,panel.at[512*xx+128*q:512*xx+128*q+128,:],rowpart(xx,z,128*q,128),CS+q,a,b)
            if xx==(1 if q<2 else 3):
                tr.send(x0,panel.at[1024+128*q:1152+128*q,:],stage.at[128*(q%2):128*(q%2)+128,:],CST+q,a,b)
        crow[q]=tr.local(x0,panel.at[128*q:128*q+128,:],rowpart(0,z,128*q,128))
    def c_forward(q):
        via=x==(1 if q<2 else 3)
        ref=stage.at[128*(q%2):128*(q%2)+128,:]
        tr.recv(via,ref,CST+q)
        a,b=at(y,core,2,z)
        tr.send(via,ref,rowpart(2,z,128*q,128),CSF+q,a,b)
    def c_have(q):
        tr.recv(x13,rowpart(x,z,128*q,128),CS+q)
        tr.recv(x2,rowpart(x,z,128*q,128),CSF+q)
        crow[q]()

    AG=tr.slots("AG",60)
    orders=[[(q+i)%4 for i in range(4)] for q in range(4)]
    def ag_send(i,qs=range(4)):
        for q in qs:
            dims=orders[q]
            xx,zz=flip(dims[i],x,z)
            a,b=at(y,core,xx,zz)
            for m,(bx,bz) in enumerate(orbit(dims[:i],x,z)):
                ref=rowpart(bx,bz,128*q,128)
                tr.send(None,ref,ref,AG+q*15+(1<<i)-1+m,a,b)
    def ag_recv(i):
        for q in range(4):
            dims=orders[q]
            xx,zz=flip(dims[i],x,z)
            for m,(bx,bz) in enumerate(orbit(dims[:i],xx,zz)):
                tr.recv(None,rowpart(bx,bz,128*q,128),AG+q*15+(1<<i)-1+m)
    def more(n):
        for e in EVENTS.get(n,[]): eval_event(e)
    table={"lead_a":lead_a,"lead_b":lead_b,"lead_c":lead_c,"lead_d":lead_d,"lead_e":lead_e,"lead_wait":lead_wait,"lead_free":lead_free,
        "b_first":b_first,"b_forward":b_forward,"b_last":b_last,"b_share":b_share,"b_done":b_done,
        "c_scatter":c_scatter,"c_forward":c_forward,"c_have":c_have,"ag_send":ag_send,"ag_recv":ag_recv}
    def eval_event(e):
        table[e[0]](*e[1:])
    chol_events(u,w,us,ws,more)
    solve_columns(col_out,u,w,uh,ul,wh,wl,yh,yl)
    blk=u[pl.ds(pl.multiple_of(jnp.minimum(c,3)*T,T),T),pl.ds(pl.multiple_of(jnp.minimum(r,3)*T,T),T)]
    l_out[...]=blk.T
    more("end")
    tr.drain(settled)


EVENTS={
    "start":[("lead_a",0),("lead_a",1),("c_scatter",1),("lead_b",0),("c_scatter",3),("lead_c",0),("lead_b",1),("c_scatter",0),
        ("lead_d",0),("lead_c",1),("c_scatter",2),("c_forward",1),("lead_e",0),("lead_d",1),("c_forward",3),("c_have",1),("ag_send",0,(1,)),("lead_wait",0)],
    "0a":[("lead_free",0),("c_forward",0),("c_have",3),("ag_send",0,(3,)),("lead_e",1),("c_forward",2),("c_have",0),("c_have",2),("ag_send",0,(0,2))],
    0:[("b_first",0),("b_first",1),("b_first",2),("b_first",3)],
    "1a":[("lead_wait",1),("ag_recv",0),("ag_send",1)],
    1:[("lead_free",1),("lead_free",2),("lead_free",3)],
    "2a":[("ag_recv",1),("ag_send",2),("b_forward",0)],
    2:[("b_forward",1)],
    3:[("b_forward",2),("b_forward",3)],
    "4a":[("ag_recv",2),("ag_send",3)],
    5:[("b_last",q) for q in range(4)]+[("b_share",q) for q in range(4)],
    7:[("b_done",q) for q in range(4)],
    "end":[("ag_recv",3)],
}


def chol_events(u,w,us,ws,more):
    H=128
    more("start")
    for K in range(4):
        ko=T*K
        if K:
            u[ko:ko+T,ko:]=u[ko:ko+T,ko:]-dotx(u[:ko,ko:ko+T],u[:ko,ko:],TN)
            u[ko:ko+T,:ko]=jnp.zeros((T,ko),F32)
        Ws=[]
        for h in range(2):
            o=ko+H*h
            block128(u[o:o+H,o:o+H],us,ws)
            more("%da"%(2*K+h))
            ii,jj=iotas(H,H)
            W=jnp.where(jj<=ii,ws[...],0.0)
            n=1024-ko
            ri,ci=iotas(H,n)
            U=jnp.where(ci>=ri+H*h,dotx(W,u[o:o+H,ko:]),0.0)
            u[o:o+H,ko:]=U
            if h==0:
                u[o+H:o+T,ko:]=u[o+H:o+T,ko:]-dotx(U[:,H:T],U,TN)
                w[K,:H,:H]=W
                w[K,:H,H:]=jnp.zeros((H,H),F32)
                L21=dotx(U[:,H:T],W,TN)
            else:
                w[K,H:,H:]=W
                w[K,H:,:H]=-dotx(W,L21)
            more(2*K+h)


def solve_columns(cols,u,w,uh,ul,wh,wl,yh,yl):
    for k in range(4):
        ks=slice(k*T,(k+1)*T)
        uh[ks,:],ul[ks,:]=split(u[ks,:])
        wh[k],wl[k]=split(w[k])
        acc=jnp.concatenate([cols[k,q] for q in range(4)],axis=1)
        if k:
            acc=acc-dot3((uh[:k*T,ks],ul[:k*T,ks]),(yh[:k*T,:],yl[:k*T,:]),TN)
        yh[ks,:],yl[ks,:]=split(dot3((wh[k],wl[k]),split(acc)))


def gather_factor(panel,strip):
    any_=pl.BlockSpec(memory_space=pl.ANY); vm=pl.BlockSpec(memory_space=pltpu.VMEM)
    full=jax.ShapeDtypeStruct((1024,1024),BF); diag=jax.ShapeDtypeStruct((4,256,256),BF)
    return pl.pallas_call(gather_factor_kernel,
        out_shape=[jax.ShapeDtypeStruct((4,2048,256),F32),jax.ShapeDtypeStruct((256,256),F32),full,full,diag,diag,full,full],
        in_specs=[any_,any_],out_specs=[any_]+[vm]*7,
        scratch_shapes=[pltpu.VMEM((1024,1024),F32),pltpu.VMEM((4,256,256),F32),pltpu.VMEM((4,4,256,256),F32)]+[pltpu.VMEM((128,128),F32)]*2
            +[pltpu.VMEM((256,256),F32),pltpu.SemaphoreType.DMA((220,)),pltpu.SemaphoreType.DMA((150,))],
        compiler_params=pltpu.CompilerParams(vmem_limit_bytes=48<<20,collective_id=0,has_side_effects=True),name="gather_factor")(panel,strip)


def per_device(kernel):
    r=lax.axis_index("row"); c=lax.axis_index("col")
    panel=kernel[:,:,0,:].reshape(2048,256)
    strip=kernel[0].transpose(1,0,2)
    rows,*rest=gather_factor(panel,strip)
    pos=jnp.stack([r,c]).astype(jnp.int32)
    return finish(pos,kernel,rows,*rest)


def solution(mesh):
    spec=P(None,"row",None,"col")
    return jax.shard_map(per_device,mesh=mesh,in_specs=(spec,),out_specs=spec,check_vma=False)
```

```python
import functools

import jax
import jax.numpy as jnp
from jax import lax
from jax.experimental import pallas as pl
from jax.experimental.pallas import tpu as pltpu
from jax.sharding import PartitionSpec as P

F32=jnp.float32; BF=jnp.bfloat16; T=256

def split(a):
    hi=a.astype(BF)
    return hi,(a-hi.astype(F32)).astype(BF)
NN=(((1,),(0,)),((),())); NT=(((1,),(1,)),((),())); TN=(((0,),(0,)),((),()))
def dot3(a,b,dims=NN):
    d=functools.partial(lax.dot_general,dimension_numbers=dims,preferred_element_type=F32)
    return d(a[0],b[0])+(d(a[0],b[1])+d(a[1],b[0]))

def finish_kernel(pos,ker,rows,l_blk,uh,ul,wh,wl,yh,yl,out,xh,xl,xp):
    t=pl.program_id(0); r=pos[0]; c=pos[1]
    n=ker.shape[0]
    for k in range(4):
        ks=slice(k*T,(k+1)*T)
        acc=rows[k]
        if k:
            acc=acc-dot3((xh[:,:k*T],xl[:,:k*T]),(uh[:k*T,ks],ul[:k*T,ks]))
        x=dot3(split(acc),(wh[k],wl[k]),NT)
        xh[:,ks],xl[:,ks]=split(x)
        xp[:,ks]=x
    for uu in range(4):
        us=slice(uu*T,(uu+1)*T)
        s=dot3((xh[...],xl[...]),(yh[:,us],yl[:,us]))
        for i in range(n):
            out[i,:,uu,:]=ker[i,:,uu,:]-s[i*T:(i+1)*T]
    @pl.when(c<4)
    def _():
        for i in range(n):
            out[i,:,0,:]=xp[i*T:(i+1)*T,pl.ds(pl.multiple_of(jnp.minimum(c,3)*T,T),T)]
    @pl.when(jnp.logical_and(t==0,r<4))
    def _():
        out[0]=jnp.zeros_like(out[0])
        @pl.when(c<4)
        def _():
            out[0,:,0,:]=l_blk[...]


def finish(pos,kernel,rows,*rest):
    n=2
    full=lambda a: pl.BlockSpec(a.shape,lambda t:(0,)*a.ndim,pipeline_mode=pl.Buffered(1))
    return pl.pallas_call(finish_kernel,grid=(8//n,),
        in_specs=[pl.BlockSpec(memory_space=pltpu.SMEM),pl.BlockSpec((n,256,4,256),lambda t:(t,0,0,0)),
                  pl.BlockSpec((4,n*256,256),lambda t:(0,t,0))]+[full(a) for a in rest],
        out_specs=pl.BlockSpec((n,256,4,256),lambda t:(t,0,0,0)),
        out_shape=jax.ShapeDtypeStruct((8,256,4,256),F32),
        scratch_shapes=[pltpu.VMEM((n*256,1024),BF)]*2+[pltpu.VMEM((n*256,1024),F32)],
        compiler_params=pltpu.CompilerParams(vmem_limit_bytes=56<<20),name="finish")(pos,kernel,rows,*rest)


HI=lax.Precision.HIGHEST
def bc(x,i,n=8): return jnp.broadcast_to(x[i:i+1,:],(n,x.shape[1]))
def dotx(a,b,dims=NN): return lax.dot_general(a,b,dims,precision=HI,preferred_element_type=F32)
def leaf(V, c0, b, u_ref, w_ref, r0, mb):
    nt=b//8; mt=mb//8
    VT=[[V[8*t:8*t+8,128*h:128*h+128] for h in range(2)] for t in range(nt)]
    refs=[u_ref,w_ref]
    for s in range(0,nt,mt):
        C=[[jnp.broadcast_to(VT[t][0][:, c0+8*s+j:c0+8*s+j+1],(8,128)) if t>=s+j//8 else None for t in range(nt)] for j in range(mb)]
        d=bc(C[0][s],0)
        for k in range(mb):
            tk=s+k//8
            ck=C[k]
            q=pltpu.reciprocal(d,approx=False)
            rs=lax.rsqrt(d)
            if k+1<mb:
                sb=bc(ck[s+(k+1)//8],(k+1)%8)
                p=bc(C[k+1][s+(k+1)//8],(k+1)%8)
                d=p-(sb*sb)*q
            m=[ck[t]*q if t>=tk else None for t in range(nt)]
            v=[bc(VT[tk][h],k%8) for h in range(2)]
            for h in range(2): refs[h][r0+8*s+k:r0+8*s+k+1,:]=(v[h]*rs)[:1]
            for j in range(k+1,mb):
                cj=bc(ck[s+j//8],j%8)
                for t in range(s+j//8,nt):
                    C[j][t]=C[j][t]-m[t]*cj
            for t in range(s+(k+1)//8,nt):
                for h in range(2):
                    VT[t][h]=VT[t][h]-m[t]*v[h]
def iotas(n,m):
    return lax.broadcasted_iota(jnp.int32,(n,m),0),lax.broadcasted_iota(jnp.int32,(n,m),1)
def block128(D,us,ws,b=32,mb=16):
    ii,jj=iotas(128,128)
    I=(ii==jj).astype(F32)
    for s in range(128//b):
        r0=s*b
        V=jnp.concatenate([D[r0:r0+b],I[r0:r0+b]],axis=1)
        if s:
            up=us[:r0,:]; wp=ws[:r0,:]
            V=V-dotx(up[:,r0:r0+b], jnp.concatenate([up,wp],axis=1),TN)
        leaf(V,r0,b,us,ws,r0,mb)


def flip(dim, x, z):
    if dim==0: return x+1-2*lax.rem(x,2),z
    if dim==1: return x,z+1-2*lax.rem(z,2)
    if dim==2: return 3-x,z
    return x,3-z


def orbit(dims, x, z):
    out=[(x,z)]
    for d in dims:
        out=out+[flip(d,a,b) for a,b in out]
    return out


class Traffic:
    def __init__(self, send_sems, recv_sems):
        self.send_sems=send_sems; self.recv_sems=recv_sems
        self.sent=[]; self.keys={}; self.next=0

    def slots(self, key, n):
        if key not in self.keys:
            self.keys[key]=self.next
            self.next+=n
        return self.keys[key]

    def send(self, cond, src, dst, sem, row, col):
        d=pltpu.make_async_remote_copy(src_ref=src,dst_ref=dst,send_sem=self.send_sems.at[len(self.sent)],recv_sem=self.recv_sems.at[sem],
            device_id={"row":row,"col":col},device_id_type=pl.DeviceIdType.MESH)
        if cond is None: d.start()
        else: pl.when(cond)(lambda: d.start())
        self.sent.append((cond,d))
        return len(self.sent)-1

    def settle(self, n, cond):
        c,d=self.sent[n]
        c=both(c,cond)
        if c is None: d.wait_send()
        else: pl.when(c)(lambda: d.wait_send())

    def local(self, cond, src, dst):
        d=pltpu.make_async_copy(src,dst,self.send_sems.at[len(self.sent)])
        if cond is None: d.start()
        else: pl.when(cond)(lambda: d.start())
        self.sent.append((None,None))
        def wait():
            if cond is None: d.wait()
            else: pl.when(cond)(lambda: d.wait())
        return wait

    def recv(self, cond, dst, sem):
        d=pltpu.make_async_copy(dst,dst,self.recv_sems.at[sem])
        if cond is None: d.wait()
        else: pl.when(cond)(lambda: d.wait())

    def drain(self, settled):
        for n,(cond,d) in enumerate(self.sent):
            if d is None or n in settled: continue
            if cond is None: d.wait_send()
            else: pl.when(cond)(lambda d=d: d.wait_send())


def both(a,b):
    return b if a is None else a if b is None else jnp.logical_and(a,b)


def gather_factor_kernel(panel,strip,row_out,l_out,uh,ul,wh,wl,yh,yl,u,w,col_out,us,ws,stage,send_sems,recv_sems):
    r=lax.axis_index("row"); c=lax.axis_index("col")
    y=r//2; core=lax.rem(r,2); x=c//4; z=lax.rem(c,4)
    up=lambda v,n=1: lax.rem(v+n,4)
    at=lambda yy,kk,xx,zz: (2*yy+kk,4*xx+zz)
    tr=Traffic(send_sems,recv_sems)
    bar=pltpu.get_barrier_semaphore()
    friends=[at(up(y,i),core,x,z) for i in (1,2,3)]+[at(y,1-core,x,z)]+[at(y,core,up(x,i),z) for i in (1,2,3)]+[at(y,core,x,up(z,i)) for i in (1,2,3)]
    for a,b in friends:
        pl.semaphore_signal(bar,inc=1,device_id={"row":a,"col":b},device_id_type=pl.DeviceIdType.MESH)
    pl.semaphore_wait(bar,len(friends))

    tile=lambda k,U,o=0,n=T: u.at[pl.ds(pl.multiple_of(k*T+o,n),n),pl.ds(pl.multiple_of(U*T,T),T)]
    rs=jnp.minimum(r,3)
    low=y<2
    x0=x==0; x13=lax.rem(x,2)==1; x2=x==2
    rowpart=lambda xx,zz,o,n: row_out.at[zz,pl.ds(pl.multiple_of(xx*512+o,128),n),:]
    kk=lambda j: 2*j+core
    parts=[[(0,0,256)],[(1,0,256),(2,0,256),(3,0,256)]]
    lead_sent=[[] for _ in range(4)]
    def pieces(g):
        for k,o,n in parts[g]:
            key=k*2+(1 if o else 0)
            yield k,o,n,core==k%2,"%d"%key
    def window(k,o,n,q):
        return u.at[pl.ds(pl.multiple_of(k*T+o+n//4*q,n//4),n//4),k*T:]
    def patch(k,o,n,q,U):
        return u.at[pl.ds(pl.multiple_of(k*T+o+n//4*q,n//4),n//4),pl.ds(pl.multiple_of(U*T,T),T)]
    own_lead=[[] for _ in parts]
    def lead_a(g):
        for k,o,n,ok,key in pieces(g):
            sem=tr.slots("LA"+key,1); m=n//4
            go=jnp.logical_and(jnp.logical_and(ok,x0),jnp.logical_and(y==k//2,z>=k))
            src=lambda q: strip.at[0,pl.ds(pl.multiple_of(o+m*q,m),m),:]
            for i in (1,2,3):
                a,b=at(up(y,i),core,x,z)
                tr.send(go,src(up(y,i)),patch(k,o,n,up(y,i),z),sem,a,b)
            own_lead[g].append(tr.local(go,src(y),patch(k,o,n,y,z)))
    def lead_b(g):
        for wait in own_lead[g]: wait()
        for k,o,n,ok,key in pieces(g):
            ref=patch(k,o,n,y,z)
            go=jnp.logical_and(ok,jnp.logical_and(x0,z>=k))
            tr.recv(jnp.logical_and(go,y!=k//2),ref,tr.slots("LA"+key,1))
            sem=tr.slots("LB"+key,1)
            for i in (1,2,3):
                a,b=at(y,core,i,z)
                lead_sent[k].append(tr.send(go,ref,ref,sem,a,b))
    def lead_c(g):
        for k,o,n,ok,key in pieces(g):
            ref=patch(k,o,n,y,z)
            go=jnp.logical_and(ok,z>=k)
            tr.recv(jnp.logical_and(go,x!=0),ref,tr.slots("LB"+key,1))
            sem=tr.slots("LC"+key,3)
            for i in (1,2,3):
                a,b=at(y,core,x,up(z,i))
                lead_sent[k].append(tr.send(go,ref,ref,sem+i-1,a,b))
    def lead_d(g):
        for k,o,n,ok,key in pieces(g):
            sem=tr.slots("LC"+key,3)
            for i in (1,2,3):
                U=up(z,4-i)
                tr.recv(jnp.logical_and(ok,U>=k),patch(k,o,n,y,U),sem+i-1)
            ref=window(k,o,n,y)
            sem=tr.slots("LD"+key,3); cs=tr.slots("LE"+key,4)
            for i in (1,2,3):
                a,b=at(up(y,i),core,x,z)
                lead_sent[k].append(tr.send(ok,ref,ref,sem+i-1,a,b))
            a,b=at(y,1-core,x,z)
            lead_sent[k].append(tr.send(ok,ref,ref,cs,a,b))
    def lead_e(g):
        for k,o,n,ok,key in pieces(g):
            sem=tr.slots("LD"+key,3); cs=tr.slots("LE"+key,4)
            for i in (1,2,3):
                ref=window(k,o,n,up(y,4-i))
                tr.recv(ok,ref,sem+i-1)
                a,b=at(y,1-core,x,z)
                lead_sent[k].append(tr.send(ok,ref,ref,cs+i,a,b))
    def lead_wait(g):
        for k,o,n,ok,key in pieces(g):
            cs=tr.slots("LE"+key,4)
            for i in range(4):
                tr.recv(jnp.logical_not(ok),window(k,o,n,up(y,4-i)),cs+i)
    def lead_free(K):
        for n in lead_sent[K]:
            tr.settle(n,None)
            settled.add(n)
    settled=set()

    B=tr.slots("B",8); BD=tr.slots("BD",8)
    own=[]
    def b_first(q):
        own.append(tr.local(low,strip.at[q],col_out.at[rs,q]))
        for i in (1,3):
            a,b=at(up(y,i),core,x,z)
            tr.send(low,strip.at[q],col_out.at[rs,q],B+jnp.minimum(y,1)*4+q,a,b)
    def b_forward(q):
        f=jnp.clip(3-y,0,1)
        tr.recv(y>=2,col_out.at[2*f+core,q],B+f*4+q)
        a,b=at(jnp.clip(5-y,0,3),core,x,z)
        tr.send(y>=2,col_out.at[2*f+core,q],col_out.at[2*f+core,q],B+f*4+q,a,b)
    def b_last(q):
        o=jnp.where(y>=2,y-2,1-y)
        tr.recv(None,col_out.at[2*o+core,q],B+o*4+q)
        own[q]()
    def b_share(q):
        a,b=at(y,1-core,x,z)
        for j in (0,1):
            tr.send(None,col_out.at[2*j+core,q],col_out.at[2*j+core,q],BD+j*4+q,a,b)
    def b_done(q):
        for j in (0,1):
            tr.recv(None,col_out.at[2*j+1-core,q],BD+j*4+q)

    CS=tr.slots("CS",4); CST=tr.slots("CST",4); CSF=tr.slots("CSF",4)
    crow={}
    def c_scatter(q):
        for xx in (1,3):
            a,b=at(y,core,xx,z)
            tr.send(x0,panel.at[512*xx+128*q:512*xx+128*q+128,:],rowpart(xx,z,128*q,128),CS+q,a,b)
            if xx==(1 if q<2 else 3):
                tr.send(x0,panel.at[1024+128*q:1152+128*q,:],stage.at[128*(q%2):128*(q%2)+128,:],CST+q,a,b)
        crow[q]=tr.local(x0,panel.at[128*q:128*q+128,:],rowpart(0,z,128*q,128))
    def c_forward(q):
        via=x==(1 if q<2 else 3)
        ref=stage.at[128*(q%2):128*(q%2)+128,:]
        tr.recv(via,ref,CST+q)
        a,b=at(y,core,2,z)
        tr.send(via,ref,rowpart(2,z,128*q,128),CSF+q,a,b)
    def c_have(q):
        tr.recv(x13,rowpart(x,z,128*q,128),CS+q)
        tr.recv(x2,rowpart(x,z,128*q,128),CSF+q)
        crow[q]()

    AG=tr.slots("AG",60)
    orders=[[(q+i)%4 for i in range(4)] for q in range(4)]
    def ag_send(i,qs=range(4)):
        for q in qs:
            dims=orders[q]
            xx,zz=flip(dims[i],x,z)
            a,b=at(y,core,xx,zz)
            for m,(bx,bz) in enumerate(orbit(dims[:i],x,z)):
                ref=rowpart(bx,bz,128*q,128)
                tr.send(None,ref,ref,AG+q*15+(1<<i)-1+m,a,b)
    def ag_recv(i):
        for q in range(4):
            dims=orders[q]
            xx,zz=flip(dims[i],x,z)
            for m,(bx,bz) in enumerate(orbit(dims[:i],xx,zz)):
                tr.recv(None,rowpart(bx,bz,128*q,128),AG+q*15+(1<<i)-1+m)
    def more(n):
        for e in EVENTS.get(n,[]): eval_event(e)
    table={"lead_a":lead_a,"lead_b":lead_b,"lead_c":lead_c,"lead_d":lead_d,"lead_e":lead_e,"lead_wait":lead_wait,"lead_free":lead_free,
        "b_first":b_first,"b_forward":b_forward,"b_last":b_last,"b_share":b_share,"b_done":b_done,
        "c_scatter":c_scatter,"c_forward":c_forward,"c_have":c_have,"ag_send":ag_send,"ag_recv":ag_recv}
    def eval_event(e):
        table[e[0]](*e[1:])
    chol_events(u,w,us,ws,more)
    solve_columns(col_out,u,w,uh,ul,wh,wl,yh,yl)
    blk=u[pl.ds(pl.multiple_of(jnp.minimum(c,3)*T,T),T),pl.ds(pl.multiple_of(jnp.minimum(r,3)*T,T),T)]
    l_out[...]=blk.T
    more("end")
    tr.drain(settled)


EVENTS={
    "start":[("lead_a",0),("lead_a",1),("c_scatter",1),("lead_b",0),("c_scatter",3),("lead_c",0),("lead_b",1),("c_scatter",0),
        ("lead_d",0),("lead_c",1),("c_scatter",2),("c_forward",1),("lead_e",0),("c_forward",3),("c_have",1),("ag_send",0,(1,)),("c_have",3),("ag_send",0,(3,)),("lead_wait",0)],
    "0a":[("lead_free",0),("lead_d",1),("c_forward",0),("c_forward",2),("c_have",0),("c_have",2),("ag_send",0,(0,2)),("lead_e",1)],
    0:[("b_first",0),("b_first",1),("b_first",2),("b_first",3)],
    "1a":[("lead_wait",1),("ag_recv",0),("ag_send",1)],
    1:[("lead_free",1),("lead_free",2),("lead_free",3),("ag_recv",1),("ag_send",2)],
    "2a":[("b_forward",0)],
    2:[("b_forward",1)],
    3:[("ag_recv",2),("ag_send",3),("b_forward",2),("b_forward",3)],
    5:[("b_last",q) for q in range(4)]+[("b_share",q) for q in range(4)],
    7:[("b_done",q) for q in range(4)],
    "end":[("ag_recv",3)],
}


def chol_events(u,w,us,ws,more):
    H=128
    more("start")
    for K in range(4):
        ko=T*K
        if K:
            u[ko:ko+T,ko:]=u[ko:ko+T,ko:]-dotx(u[:ko,ko:ko+T],u[:ko,ko:],TN)
            u[ko:ko+T,:ko]=jnp.zeros((T,ko),F32)
        Ws=[]
        for h in range(2):
            o=ko+H*h
            block128(u[o:o+H,o:o+H],us,ws)
            more("%da"%(2*K+h))
            ii,jj=iotas(H,H)
            W=jnp.where(jj<=ii,ws[...],0.0)
            n=1024-ko
            ri,ci=iotas(H,n)
            U=jnp.where(ci>=ri+H*h,dotx(W,u[o:o+H,ko:]),0.0)
            u[o:o+H,ko:]=U
            if h==0:
                u[o+H:o+T,ko:]=u[o+H:o+T,ko:]-dotx(U[:,H:T],U,TN)
                w[K,:H,:H]=W
                w[K,:H,H:]=jnp.zeros((H,H),F32)
                L21=dotx(U[:,H:T],W,TN)
            else:
                w[K,H:,H:]=W
                w[K,H:,:H]=-dotx(W,L21)
            more(2*K+h)


def solve_columns(cols,u,w,uh,ul,wh,wl,yh,yl):
    for k in range(4):
        ks=slice(k*T,(k+1)*T)
        uh[ks,:],ul[ks,:]=split(u[ks,:])
        wh[k],wl[k]=split(w[k])
        acc=jnp.concatenate([cols[k,q] for q in range(4)],axis=1)
        if k:
            acc=acc-dot3((uh[:k*T,ks],ul[:k*T,ks]),(yh[:k*T,:],yl[:k*T,:]),TN)
        yh[ks,:],yl[ks,:]=split(dot3((wh[k],wl[k]),split(acc)))


def gather_factor(panel,strip):
    any_=pl.BlockSpec(memory_space=pl.ANY); vm=pl.BlockSpec(memory_space=pltpu.VMEM)
    full=jax.ShapeDtypeStruct((1024,1024),BF); diag=jax.ShapeDtypeStruct((4,256,256),BF)
    return pl.pallas_call(gather_factor_kernel,
        out_shape=[jax.ShapeDtypeStruct((4,2048,256),F32),jax.ShapeDtypeStruct((256,256),F32),full,full,diag,diag,full,full],
        in_specs=[any_,any_],out_specs=[any_]+[vm]*7,
        scratch_shapes=[pltpu.VMEM((1024,1024),F32),pltpu.VMEM((4,256,256),F32),pltpu.VMEM((4,4,256,256),F32)]+[pltpu.VMEM((128,128),F32)]*2
            +[pltpu.VMEM((256,256),F32),pltpu.SemaphoreType.DMA((220,)),pltpu.SemaphoreType.DMA((150,))],
        compiler_params=pltpu.CompilerParams(vmem_limit_bytes=48<<20,collective_id=0,has_side_effects=True),name="gather_factor")(panel,strip)


def per_device(kernel):
    r=lax.axis_index("row"); c=lax.axis_index("col")
    panel=kernel[:,:,0,:].reshape(2048,256)
    strip=kernel[0].transpose(1,0,2)
    rows,*rest=gather_factor(panel,strip)
    pos=jnp.stack([r,c]).astype(jnp.int32)
    return finish(pos,kernel,rows,*rest)


def solution(mesh):
    spec=P(None,"row",None,"col")
    return jax.shard_map(per_device,mesh=mesh,in_specs=(spec,),out_specs=spec,check_vma=False)
```
